32 devices in a mesh: tile: 8 (over y, x, core), ens: 4 (over z).
Axes of the slice: x: 2, y: 2, z: 4, core: 2. Of those that a mesh axis runs over, the one named last changes fastest.
Arguments:
- residual: float32 [8, 64, 128], P('ens', 'tile'), may hold values from -6 to 6
- kernel: float32 [64, 8, 128], P('tile'), may hold values from 0.2 to 2
- dest_tile: int32 [64, 1], P('tile'), may hold values from 0 to 7; in each aligned block of 8 rows (0 to 7, 8 to 15, ...) at most 2 rows name the same one
- cell_ids: int32 [64, 128], P('tile'), may hold values from 0 to 8191
- wind_x: float32 [8, 8, 128, 512], P('ens', None, 'tile'), may hold values from -0.5 to 0.5
- wind_y: float32 [8, 8, 128, 512], P('ens', None, 'tile'), may hold values from -0.2 to 0.2
- mixing: float32 [8, 8, 128, 512], P('ens', None, 'tile'), may hold values from 0.01 to 0.15
- sources: int32 [16], replicated, may hold values from 0 to 65535
- gram_matrix: float32 [16, 16], replicated, as said below
Outputs:
- gradient: float32 [128, 512], P('tile', 'ens')
- coefficients: float32 [16], replicated
- adjoint: float32 [8, 8, 128, 512], P('ens', None, 'tile')
The draws below stay inside these ranges and needn't reach their ends.
Inputs may be any that keep to these rules, and one draw needn't show every extreme that they name: `dest_tile`: among the blocks held by one tile device, at most 2 share a footprint tile, and some footprint tile gets exactly 2 of them on every device. `gram_matrix`: symmetric and strictly diagonally dominant with a positive diagonal.
All inputs are finite; a program needn't handle non-finite values.
Results may differ from the reference program's by a relative error of at most 0.00013.
Values sent between devices are 32-bit elements; how exact they have to be, the bound alone decides.
A program may use at most 64 MiB of HBM per device.

```python
import math
import jax
import jax.numpy as jnp
import numpy as np
from jax import lax

CX = 16
NY = 512
LEV = 8
ROWS = 128
CAP = 2
STEPS = 6
NSRC = 16
OBS_BLOCKS = 8
NBLK = 64
NX = 128
MEMBERS = 8
N_TILE = 8


def draw_gram_matrix(key, part):
    first_key, second_key = jax.random.split(jax.random.fold_in(key, 7))
    offdiag = jax.random.uniform(first_key, (NSRC, NSRC), jnp.float32, -1.0, 1.0)
    offdiag = (offdiag + offdiag.T) * 0.05
    diagonal = 2.0 + jax.random.uniform(second_key, (NSRC,), jnp.float32)
    identity = jnp.eye(NSRC, dtype=jnp.float32)
    return offdiag * (1.0 - identity) + identity * diagonal[:, None]


def with_ends(array, stream_key, smallest, high):
    dims = array.shape
    place = [jax.random.randint(jax.random.fold_in(stream_key, axis), (), 0, dims[axis]) for axis in range(len(dims))]
    array = array.at[tuple(place)].set(smallest)
    longest = dims.index(max(dims))
    place[longest] = (place[longest] + 1) % dims[longest]
    return array.at[tuple(place)].set(high)


def level_of(own_key, extent, shards, least, high):
    loudness, own = 1.0, jax.random.fold_in(own_key, 6)
    for dim, shards_of in shards:
        steps = jnp.exp(jax.random.uniform(jax.random.fold_in(own, dim), (shards_of,), jnp.float32, least / len(shards), high / len(shards)))
        loudness = loudness * jnp.repeat(steps, extent[dim] // shards_of).reshape([-1 if axis == dim else 1 for axis in range(len(extent))])
    return loudness


def assign_block(stream_key, own, number, rows, amount, top, reach, lean):
    ranking = jax.random.permutation(stream_key, amount)
    packed, common = shares(amount, rows * top, reach, lean, True), shares(amount, rows * top, reach, lean, False)
    places = jnp.arange(amount)

    def named(sizes, turn):
        used = int((sizes > 0).sum())
        fixed = max(1, used // 4)
        moved = fixed + (places - fixed + turn * (used - fixed)) % max(1, amount - fixed)
        return jnp.zeros((amount,), jnp.int32).at[ranking[jnp.where(places < fixed, places, moved)]].set(jnp.asarray(sizes, jnp.int32))

    sizes = jnp.where(number % 4 == 0, named(packed, number // 4), named(common, number - number // 4 - 1))
    mixed = jax.random.permutation(jax.random.fold_in(own, 3), amount)
    donor, sink = mixed[0:amount // 2 * 2:2], mixed[1:amount // 2 * 2:2]
    slack = jnp.minimum(sizes[donor] - 1, reach - sizes[sink]) // 2
    slack = jnp.where((donor == ranking[0]) | (sink == ranking[0]) | (sizes[sink] == 0), 0, jnp.maximum(slack, 0))
    moved = jax.random.randint(jax.random.fold_in(own, 4), (amount // 2,), 0, 1 << 20) % (slack + 1)
    sizes = sizes.at[donor].add(-moved).at[sink].add(moved)
    labels = jnp.searchsorted(jnp.cumsum(sizes), jnp.arange(rows * top), side="right").astype(jnp.int32)
    listing = labels.reshape(top, rows).T
    listing = listing[jax.random.permutation(jax.random.fold_in(own, 1), rows)]
    turn = jax.random.randint(jax.random.fold_in(own, 2), (rows, 1), 0, top)
    return jnp.take_along_axis(listing, (jnp.arange(top)[None, :] + turn) % top, axis=1)


def shares(number_of, total, bound, skew, full):
    weights = [(1 << 20) // math.isqrt(grade ** skew) + 1 for grade in range(1, number_of + 1)]
    largest = bound if full else min(bound, max(-(-total // number_of), total * weights[0] // sum(weights)))
    least = 1 if total - largest >= number_of - 1 else 0
    counts, rest = [largest] + [least] * (number_of - 1), total - largest - least * (number_of - 1)
    while rest > 0:
        free = [i for i in range(1, number_of) if counts[i] < largest] or [i for i in range(1, number_of) if counts[i] < bound]
        mass, left = sum([weights[i] for i in free]), rest
        for i in free:
            more = min(bound - counts[i], max(1, left * weights[i] // mass), rest)
            counts[i] = counts[i] + more
            rest = rest - more
    return np.array(counts)


def scatter_about(rng, dims, spread, bound, pieces=(), kind=jnp.bfloat16):
    factor_of = level_of(rng, dims, pieces, -0.22, 0.18) if pieces else 1.0
    array = jax.random.normal(rng, dims, jnp.float32) * spread * factor_of
    return jnp.minimum(jnp.maximum(array, -bound), bound).astype(kind)


def setup_inputs(seed: int = 0) -> dict:
    keys = jax.random.split(jax.random.key(seed), 10)
    residual = scatter_about(keys[0], (MEMBERS, NBLK, ROWS), 1.0, 6.0, ((0, 4), (1, 8)), jnp.float32)
    kernel = jnp.clip(jnp.exp(math.log(2.0) - 2.3025851 * jax.random.uniform(keys[1], (NBLK, LEV, ROWS), jnp.float32) ** level_of(keys[1], (NBLK, LEV, ROWS), ((0, 8),), -0.2, 0.2)), 0.2, 2.0)
    dest_tile_keys = jax.random.split(jax.random.fold_in(keys[2], 1), NBLK // OBS_BLOCKS)
    dest_tile_turns = jax.random.permutation(jax.random.fold_in(keys[2], 3), NBLK // OBS_BLOCKS)
    dest_tile = jax.vmap(lambda own, number: assign_block(jax.random.fold_in(keys[2], 2), own, number, OBS_BLOCKS, N_TILE, 1, CAP, 2))(dest_tile_keys, dest_tile_turns).reshape((NBLK, 1))
    cell_ids = with_ends(jax.random.randint(keys[3], (NBLK, ROWS), 0, CX * NY), jax.random.fold_in(keys[3], 1), 0, (CX * NY) - 1).astype(jnp.int32)
    wind_x = jnp.clip(jax.random.uniform(keys[4], (MEMBERS, LEV, NX, NY), jnp.float32, -0.5, 0.5) * level_of(keys[4], (MEMBERS, LEV, NX, NY), ((0, 4), (2, 8)), -0.4, 0.0), -0.5, 0.5)
    wind_y = jnp.clip(jax.random.uniform(keys[5], (MEMBERS, LEV, NX, NY), jnp.float32, -0.2, 0.2) * level_of(keys[5], (MEMBERS, LEV, NX, NY), ((0, 4), (2, 8)), -0.4, 0.0), -0.2, 0.2)
    mixing = jnp.clip(jnp.exp(math.log(0.15) - 2.7080503 * jax.random.uniform(keys[6], (MEMBERS, LEV, NX, NY), jnp.float32) ** level_of(keys[6], (MEMBERS, LEV, NX, NY), ((0, 4), (2, 8)), -0.2, 0.2)), 0.01, 0.15)
    sources = with_ends(jax.random.randint(keys[7], (NSRC,), 0, NX * NY), jax.random.fold_in(keys[7], 1), 0, (NX * NY) - 1).astype(jnp.int32)
    gram_matrix = draw_gram_matrix(jax.random.fold_in(keys[9], 71), 0)
    return {"residual": residual, "kernel": kernel, "dest_tile": dest_tile, "cell_ids": cell_ids, "wind_x": wind_x, "wind_y": wind_y, "mixing": mixing, "sources": sources, "gram_matrix": gram_matrix}


def advance(adjoint, speed_x, speed_y, diffusion):
    center = adjoint[:, :, 1:-1]
    next_row = adjoint[:, :, 2:]
    prev_row = adjoint[:, :, :-2]
    along_x = jnp.maximum(speed_x, 0.0) * (next_row - center) + jnp.maximum(-speed_x, 0.0) * (prev_row - center)
    zero_col = jnp.zeros_like(center[..., :1])
    right_col = jnp.concatenate([center[..., 1:], zero_col], axis=-1)
    left_col = jnp.concatenate([zero_col, center[..., :-1]], axis=-1)
    along_y = jnp.maximum(speed_y, 0.0) * (right_col - center) + jnp.maximum(-speed_y, 0.0) * (left_col - center)
    level_flux = diffusion[:, :-1] * (center[:, 1:] - center[:, :-1])
    zero_lev = jnp.zeros_like(center[:, :1])
    vertical = jnp.concatenate([level_flux, zero_lev], axis=1) - jnp.concatenate([zero_lev, level_flux], axis=1)
    return center + along_x + along_y + vertical

def reference(residual, kernel, dest_tile, cell_ids, wind_x, wind_y, mixing, sources, gram_matrix):
    global_cells = (dest_tile[:, 0:1] * (CX * NY) + cell_ids).reshape(-1).astype(jnp.int32)

    def member_forcing(member):
        values = residual[member][:, None, :] * kernel
        flat_values = jnp.transpose(values, (1, 0, 2)).reshape(LEV, -1)
        return jnp.zeros((LEV, NX * NY), jnp.float32).at[:, global_cells].add(flat_values)
    forcing = lax.map(member_forcing, jnp.arange(MEMBERS, dtype=jnp.int32)).reshape(MEMBERS, LEV, NX, NY)
    adjoint = forcing
    totals = jnp.zeros((NX, NY), jnp.float32)
    for repeat in range(STEPS):
        padded = jnp.pad(adjoint, ((0, 0), (0, 0), (1, 1), (0, 0)))
        adjoint = advance(padded, wind_x, wind_y, mixing)
        totals = totals + jnp.sum(adjoint[:, 0], axis=0)
    picked = totals.reshape(-1)[sources]
    factor = jnp.linalg.cholesky(gram_matrix)
    coefficients = jax.scipy.linalg.cho_solve((factor, True), picked)
    return (totals, coefficients, adjoint)
```

```python
import functools

import jax
import jax.numpy as jnp
from jax import lax
from jax.experimental import pallas as pl
from jax.experimental.pallas import tpu as pltpu
from jax.sharding import PartitionSpec as P

CAP = 2
STEPS = 6
HALO = 2
GROUP = 8
LANES = 128


def roll(array, shift, axis):
    return pltpu.roll(array, shift % array.shape[axis], axis=axis)


def body(
    dims,
    dest_ref,
    sources_ref,
    residual_ref,
    kernel_ref,
    cells_ref,
    gram_ref,
    wx_ref,
    wy_ref,
    mix_ref,
    grad_ref,
    coef_ref,
    adj_ref,
    raw,
    coefs,
    states,
    total,
    outbuf,
    send_obs,
    recv_obs,
    left_hi,
    left_lo,
    right_hot,
    forcing,
    level0,
    picks,
    send_sum,
    recv_sum,
    send_pick,
    recv_pick,
    augmented,
    local_sem,
    obs_send,
    obs_recv,
    edge_send,
    edge_recv,
    halo_send,
    halo_recv,
    sum_send,
    sum_recv,
    pick_send,
    pick_recv,
    out_sem,
):
    tiles, groups, members, levels, rows, columns, blocks = dims
    width = columns // groups
    strips = columns // LANES
    nsrc = gram_ref.shape[0]
    me = lax.axis_index("tile")
    mine = lax.axis_index("ens")
    depth = members * levels
    log_columns = columns.bit_length() - 1

    loads = []
    for which, source in enumerate((wx_ref, wy_ref, mix_ref)):
        for j in range(strips):
            copy = pltpu.make_async_copy(
                source.at[:, pl.ds(j * LANES, LANES)],
                raw.at[which, j],
                local_sem.at[which, j],
            )
            copy.start()
            loads.append(copy)

    barrier = pltpu.get_barrier_semaphore()

    def greet_tile(d, carry):
        peer = lax.rem(me + d, tiles)
        pl.semaphore_signal(barrier, inc=1, device_id={"tile": peer})
        return carry

    def greet_ens(d, carry):
        peer = lax.rem(mine + d, groups)
        pl.semaphore_signal(barrier, inc=1, device_id={"ens": peer})
        return carry

    lax.fori_loop(1, tiles, greet_tile, 0)
    lax.fori_loop(1, groups, greet_ens, 0)

    def fill(tile, carry):
        def look(b, found):
            first, second = found
            here = dest_ref[b, 0] == tile
            second = jnp.where(here & (first >= 0) & (second < 0), b, second)
            first = jnp.where(here & (first < 0), b, first)
            return first, second

        none = jnp.int32(-1)
        found = lax.fori_loop(0, blocks, look, (none, none), unroll=min(blocks, 8))
        for c in range(CAP):
            block = jnp.maximum(found[c], 0)
            held = found[c] >= 0
            send_obs[tile, c * levels : (c + 1) * levels, :] = kernel_ref[block]
            base = CAP * levels + c * (members + 2)
            for m in range(members):
                part = residual_ref[m, pl.ds(block, 1), :]
                send_obs[tile, base + m : base + m + 1, :] = jnp.where(held, part, 0.0)
            ids = cells_ref[pl.ds(block, 1), :].astype(jnp.float32)
            send_obs[tile, base + members : base + members + 1, :] = ids
        return carry

    lax.fori_loop(0, tiles, fill, 0)

    pl.semaphore_wait(barrier, tiles + groups - 2)

    def obs_copy(d):
        peer = lax.rem(me + d, tiles)
        return pltpu.make_async_remote_copy(
            src_ref=send_obs.at[peer],
            dst_ref=recv_obs.at[me],
            send_sem=obs_send.at[d],
            recv_sem=obs_recv.at[d],
            device_id={"tile": peer},
        )

    def start_obs(d, carry):
        obs_copy(d).start()
        return carry

    lax.fori_loop(1, tiles, start_obs, 0)
    recv_obs[me] = send_obs[me]

    for t in range(0, STEPS + 1):

        @pl.when(me == 0)
        def _():
            states[t, 0:HALO] = jnp.zeros((HALO, members, levels, columns), jnp.float32)

        @pl.when(me == tiles - 1)
        def _():
            states[t, HALO + rows :] = jnp.zeros((HALO, members, levels, columns), jnp.float32)

    edge = HALO - 1
    if edge:

        @pl.when(me == 0)
        def _():
            coefs[0:edge] = jnp.zeros((edge,) + coefs.shape[1:], jnp.float32)

        @pl.when(me == tiles - 1)
        def _():
            coefs[edge + rows :] = jnp.zeros((edge,) + coefs.shape[1:], jnp.float32)

    for copy in loads:
        copy.wait()

    level_iota = lax.broadcasted_iota(jnp.int32, (levels, LANES), 0)
    lane_iota = lax.broadcasted_iota(jnp.int32, (levels, LANES), 1)

    def prepare(x, carry):
        for m in range(members):
            at = pl.ds(m * levels * rows + x, levels, stride=rows)
            for j in range(strips):
                wx = raw[0, j, at, :]
                wy = raw[1, j, at, :]
                mixing = raw[2, j, at, :]
                center = 1.0 - jnp.abs(wx) - jnp.abs(wy)
                if j == 0:
                    wy = jnp.where((lane_iota == 0) & (wy < 0.0), 0.0, wy)
                if j == strips - 1:
                    wy = jnp.where((lane_iota == LANES - 1) & (wy > 0.0), 0.0, wy)
                mixing = jnp.where(level_iota == levels - 1, 0.0, mixing)
                lanes = slice(j * LANES, (j + 1) * LANES)
                coefs[edge + x, 0, m, :, lanes] = center
                coefs[edge + x, 1, m, :, lanes] = wx
                coefs[edge + x, 2, m, :, lanes] = wy
                coefs[edge + x, 3, m, :, lanes] = mixing
        return carry

    lax.fori_loop(0, rows, prepare, 0)

    def edge_copy(upward):
        if upward:
            return pltpu.make_async_remote_copy(
                src_ref=coefs.at[pl.ds(rows, edge)],
                dst_ref=coefs.at[pl.ds(0, edge)],
                send_sem=edge_send.at[0],
                recv_sem=edge_recv.at[0],
                device_id={"tile": me + 1},
            )
        return pltpu.make_async_remote_copy(
            src_ref=coefs.at[pl.ds(edge, edge)],
            dst_ref=coefs.at[pl.ds(edge + rows, edge)],
            send_sem=edge_send.at[1],
            recv_sem=edge_recv.at[1],
            device_id={"tile": me - 1},
        )

    def halo_copy(t, upward):
        n = t // HALO
        if upward:
            return pltpu.make_async_remote_copy(
                src_ref=states.at[t, pl.ds(rows, HALO)],
                dst_ref=states.at[t, pl.ds(0, HALO)],
                send_sem=halo_send.at[0, n],
                recv_sem=halo_recv.at[0, n],
                device_id={"tile": me + 1},
            )
        return pltpu.make_async_remote_copy(
            src_ref=states.at[t, pl.ds(HALO, HALO)],
            dst_ref=states.at[t, pl.ds(HALO + rows, HALO)],
            send_sem=halo_send.at[1, n],
            recv_sem=halo_recv.at[1, n],
            device_id={"tile": me - 1},
        )

    def start_both(make):
        @pl.when(me < tiles - 1)
        def _():
            make(True).start()

        @pl.when(me > 0)
        def _():
            make(False).start()

    def await_both(make):
        @pl.when(me > 0)
        def _():
            make(True).wait_recv()

        @pl.when(me < tiles - 1)
        def _():
            make(False).wait_recv()

    def drain_both(make):
        @pl.when(me < tiles - 1)
        def _():
            make(True).wait_send()

        @pl.when(me > 0)
        def _():
            make(False).wait_send()

    if edge:
        start_both(edge_copy)

    row_iota = lax.broadcasted_iota(jnp.int32, (nsrc, LANES), 0)
    col_iota = lax.broadcasted_iota(jnp.int32, (nsrc, LANES), 1)
    augmented[...] = jnp.where(row_iota == col_iota, 1.0, 0.0)
    augmented[:, nsrc : 2 * nsrc] = gram_ref[...]
    table = augmented[...]
    for i in range(nsrc):
        pivot = table[i : i + 1, :]
        scaled = pivot / table[i : i + 1, nsrc + i : nsrc + i + 1]
        column = table[:, nsrc + i : nsrc + i + 1]
        table = jnp.where(row_iota == i, scaled, table - column * scaled)
    augmented[...] = table

    def await_obs(d, carry):
        obs_copy(d).wait()
        return carry

    lax.fori_loop(1, tiles, await_obs, 0)

    group = min(GROUP, tiles)
    part_rows = LANES * CAP
    cell_rows = lax.broadcasted_iota(jnp.int32, (rows, depth, LANES), 0)
    cell_cols = lax.broadcasted_iota(jnp.int32, (columns, LANES), 0)

    def place(g, carry):
        for s in range(group):
            block = recv_obs[g * group + s]
            for c in range(CAP):
                at = s * part_rows + c * LANES
                base = CAP * levels + c * (members + 2)
                weights = block[c * levels : (c + 1) * levels]
                values = jnp.concatenate(
                    [weights * block[base + m : base + m + 1] for m in range(members)], axis=0
                )
                ids = block[base + members : base + members + 1].astype(jnp.int32)
                row = jnp.right_shift(ids, log_columns)
                col = jnp.bitwise_and(ids, columns - 1)
                high = values.astype(jnp.bfloat16).astype(jnp.float32)
                low = values - high
                inside = cell_rows == row[None]
                shape = (rows * depth, LANES)
                left_hi[:, at : at + LANES] = (
                    jnp.where(inside, high[None], 0.0).reshape(shape).astype(jnp.bfloat16)
                )
                left_lo[:, at : at + LANES] = (
                    jnp.where(inside, low[None], 0.0).reshape(shape).astype(jnp.bfloat16)
                )
                right_hot[:, at : at + LANES] = jnp.where(cell_cols == col, 1.0, 0.0).astype(
                    jnp.bfloat16
                )
        numbers = (((1,), (1,)), ((), ()))
        hot = right_hot[...]
        placed = lax.dot_general(left_hi[...], hot, numbers, preferred_element_type=jnp.float32)
        placed += lax.dot_general(left_lo[...], hot, numbers, preferred_element_type=jnp.float32)
        if group == tiles:
            forcing[...] = placed
        else:
            forcing[...] += placed
        return carry

    if group == tiles:
        place(0, 0)
    else:
        forcing[...] = jnp.zeros_like(forcing)
        lax.fori_loop(0, tiles // group, place, 0)
    states[0, HALO : HALO + rows] = forcing[...].reshape(rows, members, levels, columns)

    for t in range(STEPS):
        part = t % HALO
        if part == 0:
            start_both(functools.partial(halo_copy, t))
            if t == 0 and edge:
                await_both(edge_copy)
            await_both(functools.partial(halo_copy, t))
        reach = HALO - 1 - part
        last = t == STEPS - 1

        def advance(r, carry):
            summed = None
            for m in range(members):
                here = states[t, r, m]
                above = states[t, r + 1, m]
                below = states[t, r - 1, m]
                center = coefs[r - 1, 0, m]
                wx = coefs[r - 1, 1, m]
                wy = coefs[r - 1, 2, m]
                mixing = coefs[r - 1, 3, m]
                right = roll(here, -1, 1)
                left = roll(here, 1, 1)
                flux = mixing * (roll(here, -1, 0) - here)
                new = center * here
                new += jnp.abs(wx) * jnp.where(wx > 0.0, above, below)
                new += jnp.abs(wy) * jnp.where(wy > 0.0, right, left)
                new += flux - roll(flux, 1, 0)
                if last:
                    at = pl.ds(m * levels * rows + r - HALO, levels, stride=rows)
                    for j in range(strips):
                        outbuf[j, at, :] = new[:, j * LANES : (j + 1) * LANES]
                else:
                    states[t + 1, r, m] = new
                summed = new if summed is None else summed + new
            if t > 0:
                summed = summed + total[r]
            total[r] = summed
            return carry

        lax.fori_loop(HALO - reach, HALO + rows + reach, advance, 0)

    stores = []
    for j in range(strips):
        copy = pltpu.make_async_copy(
            outbuf.at[j], adj_ref.at[:, pl.ds(j * LANES, LANES)], out_sem.at[j]
        )
        copy.start()
        stores.append(copy)

    for x in range(rows):
        level0[x : x + 1, :] = total[HALO + x, 0:1, :]
    for e in range(groups):
        send_sum[e, 0:rows, :] = level0[:, e * width : (e + 1) * width]
    wide_iota = lax.broadcasted_iota(jnp.int32, (1, columns), 1)
    for s in range(nsrc):
        place_of = sources_ref[s]
        row = jnp.right_shift(place_of, log_columns) - me * rows
        col = jnp.bitwise_and(place_of, columns - 1)
        inside = (row >= 0) & (row < rows)
        line = level0[pl.ds(jnp.clip(row, 0, rows - 1), 1), :]
        picks[s : s + 1, :] = jnp.where(wide_iota == jnp.where(inside, col, -1), line, 0.0)
    found = jnp.sum(picks[...], axis=1, keepdims=True)
    found = jnp.broadcast_to(found, (nsrc, width))
    for e in range(groups):
        send_sum[e, rows : rows + nsrc, :] = found

    def sum_copy(d):
        peer = lax.rem(mine + d, groups)
        return pltpu.make_async_remote_copy(
            src_ref=send_sum.at[peer],
            dst_ref=recv_sum.at[mine],
            send_sem=sum_send.at[d],
            recv_sem=sum_recv.at[d],
            device_id={"ens": peer},
        )

    for d in range(1, groups):
        sum_copy(d).start()
    recv_sum[mine] = send_sum[mine]
    for d in range(1, groups):
        sum_copy(d).wait()
    summed = recv_sum[0]
    for e in range(1, groups):
        summed = summed + recv_sum[e]
    grad_ref[...] = summed[0:rows]
    send_pick[...] = summed[rows : rows + nsrc]

    def pick_copy(d):
        peer = lax.rem(me + d, tiles)
        return pltpu.make_async_remote_copy(
            src_ref=send_pick,
            dst_ref=recv_pick.at[me],
            send_sem=pick_send.at[d],
            recv_sem=pick_recv.at[d],
            device_id={"tile": peer},
        )

    def start_pick(d, carry):
        pick_copy(d).start()
        return carry

    def await_pick(d, carry):
        pick_copy(d).wait()
        return carry

    lax.fori_loop(1, tiles, start_pick, 0)
    recv_pick[me] = send_pick[...]

    if edge:
        drain_both(edge_copy)
    for t in range(0, STEPS, HALO):
        drain_both(functools.partial(halo_copy, t))
    for copy in stores:
        copy.wait()

    lax.fori_loop(1, tiles, await_pick, 0)

    def gather(i, picked):
        return picked + recv_pick[i]

    picked = lax.fori_loop(1, tiles, gather, recv_pick[0])
    solved = jnp.sum(augmented[...] * picked, axis=0, keepdims=True)
    coef_ref[...] = solved[:, 0:nsrc]


def per_device(residual, kernel, dest_tile, cell_ids, wind_x, wind_y, mixing, sources, gram_matrix):
    tiles, groups = lax.axis_size("tile"), lax.axis_size("ens")
    members, levels, rows, columns = wind_x.shape
    blocks = cell_ids.shape[0]
    nsrc = gram_matrix.shape[0]
    strips = columns // LANES
    width = columns // groups
    flat = (members * levels * rows, columns)
    dims = (tiles, groups, members, levels, rows, columns, blocks)
    edge_rows = rows + 2 * (HALO - 1)
    state_rows = rows + 2 * HALO
    rounds = -(-STEPS // HALO)
    obs_rows = CAP * (levels + members + 2)
    span = min(GROUP, tiles) * CAP * LANES
    smem = pl.BlockSpec(memory_space=pltpu.SMEM)
    vmem = pl.BlockSpec(memory_space=pltpu.VMEM)
    anywhere = pl.BlockSpec(memory_space=pl.ANY)
    f32, bf16 = jnp.float32, jnp.bfloat16
    dma = pltpu.SemaphoreType.DMA
    gradient, coefficients, adjoint = pl.pallas_call(
        functools.partial(body, dims),
        out_shape=(
            jax.ShapeDtypeStruct((rows, width), f32),
            jax.ShapeDtypeStruct((1, nsrc), f32),
            jax.ShapeDtypeStruct(flat, f32),
        ),
        in_specs=[smem, smem, vmem, vmem, vmem, vmem, anywhere, anywhere, anywhere],
        out_specs=(vmem, vmem, anywhere),
        scratch_shapes=[
            pltpu.VMEM((3, strips, flat[0], LANES), f32),
            pltpu.VMEM((edge_rows, 4, members, levels, columns), f32),
            pltpu.VMEM((STEPS + 1, state_rows, members, levels, columns), f32),
            pltpu.VMEM((state_rows, levels, columns), f32),
            pltpu.VMEM((strips, flat[0], LANES), f32),
            pltpu.VMEM((tiles, obs_rows, LANES), f32),
            pltpu.VMEM((tiles, obs_rows, LANES), f32),
            pltpu.VMEM((rows * members * levels, span), bf16),
            pltpu.VMEM((rows * members * levels, span), bf16),
            pltpu.VMEM((columns, span), bf16),
            pltpu.VMEM((rows * members * levels, columns), f32),
            pltpu.VMEM((rows, columns), f32),
            pltpu.VMEM((nsrc, columns), f32),
            pltpu.VMEM((groups, rows + nsrc, width), f32),
            pltpu.VMEM((groups, rows + nsrc, width), f32),
            pltpu.VMEM((nsrc, width), f32),
            pltpu.VMEM((tiles, nsrc, width), f32),
            pltpu.VMEM((nsrc, LANES), f32),
            dma((3, strips)),
            dma((tiles,)),
            dma((tiles,)),
            dma((2,)),
            dma((2,)),
            dma((2, rounds)),
            dma((2, rounds)),
            dma((groups,)),
            dma((groups,)),
            dma((tiles,)),
            dma((tiles,)),
            dma((strips,)),
        ],
        compiler_params=pltpu.CompilerParams(
            collective_id=0, has_side_effects=True, vmem_limit_bytes=40 * 1024 * 1024
        ),
        cost_estimate=pl.CostEstimate(
            flops=1_000_000_000, bytes_accessed=2_200_000, transcendentals=0
        ),
    )(
        dest_tile,
        sources,
        residual,
        kernel,
        cell_ids,
        gram_matrix,
        wind_x.reshape(flat),
        wind_y.reshape(flat),
        mixing.reshape(flat),
    )
    return gradient, coefficients.reshape(nsrc), adjoint.reshape(wind_x.shape)


def solution(mesh):
    in_specs = (
        P("ens", "tile", None),
        P("tile", None, None),
        P("tile", None),
        P("tile", None),
        P("ens", None, "tile", None),
        P("ens", None, "tile", None),
        P("ens", None, "tile", None),
        P(),
        P(),
    )
    out_specs = (P("tile", "ens"), P(), P("ens", None, "tile", None))
    return jax.shard_map(
        per_device, mesh=mesh, in_specs=in_specs, out_specs=out_specs, check_vma=False
    )
```

```python
import functools

import jax
import jax.numpy as jnp
from jax import lax
from jax.experimental import pallas as pl
from jax.experimental.pallas import tpu as pltpu
from jax.sharding import PartitionSpec as P

CAP = 2
STEPS = 6
HALO = 2
GROUP = 8
LANES = 128


def roll(array, shift, axis):
    return pltpu.roll(array, shift % array.shape[axis], axis=axis)


def body(
    dims,
    dest_ref,
    sources_ref,
    residual_hbm,
    kernel_hbm,
    cells_hbm,
    gram_hbm,
    wx_ref,
    wy_ref,
    mix_ref,
    grad_ref,
    coef_ref,
    adj_ref,
    residual_ref,
    kernel_ref,
    cells_ref,
    gram_ref,
    raw,
    coefs,
    states,
    total,
    outbuf,
    send_obs,
    recv_obs,
    left_hi,
    left_lo,
    right_hot,
    forcing,
    level0,
    picks,
    send_sum,
    recv_sum,
    send_pick,
    recv_pick,
    augmented,
    small_sem,
    local_sem,
    obs_send,
    obs_recv,
    edge_send,
    edge_recv,
    halo_send,
    halo_recv,
    sum_send,
    sum_recv,
    pick_send,
    pick_recv,
    out_sem,
):
    tiles, groups, members, levels, rows, columns, blocks = dims
    width = columns // groups
    strips = columns // LANES
    nsrc = gram_ref.shape[0]
    me = lax.axis_index("tile")
    mine = lax.axis_index("ens")
    depth = members * levels
    log_columns = columns.bit_length() - 1

    smalls = []
    pairs = (
        (residual_hbm, residual_ref),
        (kernel_hbm, kernel_ref),
        (cells_hbm, cells_ref),
        (gram_hbm, gram_ref),
    )
    for which, (source, target) in enumerate(pairs):
        copy = pltpu.make_async_copy(source, target, small_sem.at[which])
        copy.start()
        smalls.append(copy)

    loads = []
    for which, source in enumerate((wx_ref, wy_ref, mix_ref)):
        for j in range(strips):
            copy = pltpu.make_async_copy(
                source.at[:, pl.ds(j * LANES, LANES)],
                raw.at[which, j],
                local_sem.at[which, j],
            )
            copy.start()
            loads.append(copy)

    barrier = pltpu.get_barrier_semaphore()

    def greet_tile(d, carry):
        peer = lax.rem(me + d, tiles)
        pl.semaphore_signal(barrier, inc=1, device_id={"tile": peer})
        return carry

    def greet_ens(d, carry):
        peer = lax.rem(mine + d, groups)
        pl.semaphore_signal(barrier, inc=1, device_id={"ens": peer})
        return carry

    lax.fori_loop(1, tiles, greet_tile, 0)
    lax.fori_loop(1, groups, greet_ens, 0)

    for copy in smalls:
        copy.wait()

    def fill(tile, carry):
        def look(b, found):
            first, second = found
            here = dest_ref[b, 0] == tile
            second = jnp.where(here & (first >= 0) & (second < 0), b, second)
            first = jnp.where(here & (first < 0), b, first)
            return first, second

        none = jnp.int32(-1)
        found = lax.fori_loop(0, blocks, look, (none, none), unroll=min(blocks, 8))
        for c in range(CAP):
            block = jnp.maximum(found[c], 0)
            held = found[c] >= 0
            send_obs[tile, c * levels : (c + 1) * levels, :] = kernel_ref[block]
            base = CAP * levels + c * (members + 2)
            for m in range(members):
                part = residual_ref[m, pl.ds(block, 1), :]
                send_obs[tile, base + m : base + m + 1, :] = jnp.where(held, part, 0.0)
            ids = cells_ref[pl.ds(block, 1), :].astype(jnp.float32)
            send_obs[tile, base + members : base + members + 1, :] = ids
        return carry

    lax.fori_loop(0, tiles, fill, 0)

    pl.semaphore_wait(barrier, tiles + groups - 2)

    def obs_copy(d):
        peer = lax.rem(me + d, tiles)
        return pltpu.make_async_remote_copy(
            src_ref=send_obs.at[peer],
            dst_ref=recv_obs.at[me],
            send_sem=obs_send.at[d],
            recv_sem=obs_recv.at[d],
            device_id={"tile": peer},
        )

    def start_obs(d, carry):
        obs_copy(d).start()
        return carry

    lax.fori_loop(1, tiles, start_obs, 0)
    recv_obs[me] = send_obs[me]

    for t in range(0, STEPS + 1):

        @pl.when(me == 0)
        def _():
            states[t, 0:HALO] = jnp.zeros((HALO, members, levels, columns), jnp.float32)

        @pl.when(me == tiles - 1)
        def _():
            states[t, HALO + rows :] = jnp.zeros((HALO, members, levels, columns), jnp.float32)

    edge = HALO - 1
    if edge:

        @pl.when(me == 0)
        def _():
            coefs[0:edge] = jnp.zeros((edge,) + coefs.shape[1:], jnp.float32)

        @pl.when(me == tiles - 1)
        def _():
            coefs[edge + rows :] = jnp.zeros((edge,) + coefs.shape[1:], jnp.float32)

    for copy in loads:
        copy.wait()

    level_iota = lax.broadcasted_iota(jnp.int32, (levels, LANES), 0)
    lane_iota = lax.broadcasted_iota(jnp.int32, (levels, LANES), 1)

    def prepare(x, carry):
        for m in range(members):
            at = pl.ds(m * levels * rows + x, levels, stride=rows)
            for j in range(strips):
                wx = raw[0, j, at, :]
                wy = raw[1, j, at, :]
                mixing = raw[2, j, at, :]
                center = 1.0 - jnp.abs(wx) - jnp.abs(wy)
                if j == 0:
                    wy = jnp.where((lane_iota == 0) & (wy < 0.0), 0.0, wy)
                if j == strips - 1:
                    wy = jnp.where((lane_iota == LANES - 1) & (wy > 0.0), 0.0, wy)
                mixing = jnp.where(level_iota == levels - 1, 0.0, mixing)
                lanes = slice(j * LANES, (j + 1) * LANES)
                coefs[edge + x, 0, m, :, lanes] = center
                coefs[edge + x, 1, m, :, lanes] = wx
                coefs[edge + x, 2, m, :, lanes] = wy
                coefs[edge + x, 3, m, :, lanes] = mixing
        return carry

    lax.fori_loop(0, rows, prepare, 0)

    def edge_copy(upward):
        if upward:
            return pltpu.make_async_remote_copy(
                src_ref=coefs.at[pl.ds(rows, edge)],
                dst_ref=coefs.at[pl.ds(0, edge)],
                send_sem=edge_send.at[0],
                recv_sem=edge_recv.at[0],
                device_id={"tile": me + 1},
            )
        return pltpu.make_async_remote_copy(
            src_ref=coefs.at[pl.ds(edge, edge)],
            dst_ref=coefs.at[pl.ds(edge + rows, edge)],
            send_sem=edge_send.at[1],
            recv_sem=edge_recv.at[1],
            device_id={"tile": me - 1},
        )

    def halo_copy(t, upward):
        n = t // HALO
        if upward:
            return pltpu.make_async_remote_copy(
                src_ref=states.at[t, pl.ds(rows, HALO)],
                dst_ref=states.at[t, pl.ds(0, HALO)],
                send_sem=halo_send.at[0, n],
                recv_sem=halo_recv.at[0, n],
                device_id={"tile": me + 1},
            )
        return pltpu.make_async_remote_copy(
            src_ref=states.at[t, pl.ds(HALO, HALO)],
            dst_ref=states.at[t, pl.ds(HALO + rows, HALO)],
            send_sem=halo_send.at[1, n],
            recv_sem=halo_recv.at[1, n],
            device_id={"tile": me - 1},
        )

    def start_both(make):
        @pl.when(me < tiles - 1)
        def _():
            make(True).start()

        @pl.when(me > 0)
        def _():
            make(False).start()

    def await_both(make):
        @pl.when(me > 0)
        def _():
            make(True).wait_recv()

        @pl.when(me < tiles - 1)
        def _():
            make(False).wait_recv()

    def drain_both(make):
        @pl.when(me < tiles - 1)
        def _():
            make(True).wait_send()

        @pl.when(me > 0)
        def _():
            make(False).wait_send()

    if edge:
        start_both(edge_copy)

    row_iota = lax.broadcasted_iota(jnp.int32, (nsrc, LANES), 0)
    col_iota = lax.broadcasted_iota(jnp.int32, (nsrc, LANES), 1)
    augmented[...] = jnp.where(row_iota == col_iota, 1.0, 0.0)
    augmented[:, nsrc : 2 * nsrc] = gram_ref[...]
    table = augmented[...]
    for i in range(nsrc):
        pivot = table[i : i + 1, :]
        scaled = pivot / table[i : i + 1, nsrc + i : nsrc + i + 1]
        column = table[:, nsrc + i : nsrc + i + 1]
        table = jnp.where(row_iota == i, scaled, table - column * scaled)
    augmented[...] = table

    def await_obs(d, carry):
        obs_copy(d).wait()
        return carry

    lax.fori_loop(1, tiles, await_obs, 0)

    group = min(GROUP, tiles)
    part_rows = LANES * CAP
    cell_rows = lax.broadcasted_iota(jnp.int32, (rows, depth, LANES), 0)
    cell_cols = lax.broadcasted_iota(jnp.int32, (columns, LANES), 0)

    def place(g, carry):
        for s in range(group):
            block = recv_obs[g * group + s]
            for c in range(CAP):
                at = s * part_rows + c * LANES
                base = CAP * levels + c * (members + 2)
                weights = block[c * levels : (c + 1) * levels]
                values = jnp.concatenate(
                    [weights * block[base + m : base + m + 1] for m in range(members)], axis=0
                )
                ids = block[base + members : base + members + 1].astype(jnp.int32)
                row = jnp.right_shift(ids, log_columns)
                col = jnp.bitwise_and(ids, columns - 1)
                high = values.astype(jnp.bfloat16).astype(jnp.float32)
                low = values - high
                inside = cell_rows == row[None]
                shape = (rows * depth, LANES)
                left_hi[:, at : at + LANES] = (
                    jnp.where(inside, high[None], 0.0).reshape(shape).astype(jnp.bfloat16)
                )
                left_lo[:, at : at + LANES] = (
                    jnp.where(inside, low[None], 0.0).reshape(shape).astype(jnp.bfloat16)
                )
                right_hot[:, at : at + LANES] = jnp.where(cell_cols == col, 1.0, 0.0).astype(
                    jnp.bfloat16
                )
        numbers = (((1,), (1,)), ((), ()))
        hot = right_hot[...]
        placed = lax.dot_general(left_hi[...], hot, numbers, preferred_element_type=jnp.float32)
        placed += lax.dot_general(left_lo[...], hot, numbers, preferred_element_type=jnp.float32)
        if group == tiles:
            forcing[...] = placed
        else:
            forcing[...] += placed
        return carry

    if group == tiles:
        place(0, 0)
    else:
        forcing[...] = jnp.zeros_like(forcing)
        lax.fori_loop(0, tiles // group, place, 0)
    states[0, HALO : HALO + rows] = forcing[...].reshape(rows, members, levels, columns)

    for t in range(STEPS):
        part = t % HALO
        if part == 0:
            start_both(functools.partial(halo_copy, t))
            if t == 0 and edge:
                await_both(edge_copy)
            await_both(functools.partial(halo_copy, t))
        reach = HALO - 1 - part
        last = t == STEPS - 1

        def advance(r, carry):
            summed = None
            for m in range(members):
                here = states[t, r, m]
                above = states[t, r + 1, m]
                below = states[t, r - 1, m]
                center = coefs[r - 1, 0, m]
                wx = coefs[r - 1, 1, m]
                wy = coefs[r - 1, 2, m]
                mixing = coefs[r - 1, 3, m]
                right = roll(here, -1, 1)
                left = roll(here, 1, 1)
                flux = mixing * (roll(here, -1, 0) - here)
                new = center * here
                new += jnp.abs(wx) * jnp.where(wx > 0.0, above, below)
                new += jnp.abs(wy) * jnp.where(wy > 0.0, right, left)
                new += flux - roll(flux, 1, 0)
                if last:
                    at = pl.ds(m * levels * rows + r - HALO, levels, stride=rows)
                    for j in range(strips):
                        outbuf[j, at, :] = new[:, j * LANES : (j + 1) * LANES]
                else:
                    states[t + 1, r, m] = new
                summed = new if summed is None else summed + new
            if t > 0:
                summed = summed + total[r]
            total[r] = summed
            return carry

        lax.fori_loop(HALO - reach, HALO + rows + reach, advance, 0)

    stores = []
    for j in range(strips):
        copy = pltpu.make_async_copy(
            outbuf.at[j], adj_ref.at[:, pl.ds(j * LANES, LANES)], out_sem.at[j]
        )
        copy.start()
        stores.append(copy)

    for x in range(rows):
        level0[x : x + 1, :] = total[HALO + x, 0:1, :]
    for e in range(groups):
        send_sum[e, 0:rows, :] = level0[:, e * width : (e + 1) * width]
    wide_iota = lax.broadcasted_iota(jnp.int32, (1, columns), 1)
    for s in range(nsrc):
        place_of = sources_ref[s]
        row = jnp.right_shift(place_of, log_columns) - me * rows
        col = jnp.bitwise_and(place_of, columns - 1)
        inside = (row >= 0) & (row < rows)
        line = level0[pl.ds(jnp.clip(row, 0, rows - 1), 1), :]
        picks[s : s + 1, :] = jnp.where(wide_iota == jnp.where(inside, col, -1), line, 0.0)
    found = jnp.sum(picks[...], axis=1, keepdims=True)
    found = jnp.broadcast_to(found, (nsrc, width))
    for e in range(groups):
        send_sum[e, rows : rows + nsrc, :] = found

    def sum_copy(d):
        peer = lax.rem(mine + d, groups)
        return pltpu.make_async_remote_copy(
            src_ref=send_sum.at[peer],
            dst_ref=recv_sum.at[mine],
            send_sem=sum_send.at[d],
            recv_sem=sum_recv.at[d],
            device_id={"ens": peer},
        )

    for d in range(1, groups):
        sum_copy(d).start()
    recv_sum[mine] = send_sum[mine]
    for d in range(1, groups):
        sum_copy(d).wait()
    summed = recv_sum[0]
    for e in range(1, groups):
        summed = summed + recv_sum[e]
    grad_ref[...] = summed[0:rows]
    send_pick[...] = summed[rows : rows + nsrc]

    def pick_copy(d):
        peer = lax.rem(me + d, tiles)
        return pltpu.make_async_remote_copy(
            src_ref=send_pick,
            dst_ref=recv_pick.at[me],
            send_sem=pick_send.at[d],
            recv_sem=pick_recv.at[d],
            device_id={"tile": peer},
        )

    def start_pick(d, carry):
        pick_copy(d).start()
        return carry

    def await_pick(d, carry):
        pick_copy(d).wait()
        return carry

    lax.fori_loop(1, tiles, start_pick, 0)
    recv_pick[me] = send_pick[...]

    if edge:
        drain_both(edge_copy)
    for t in range(0, STEPS, HALO):
        drain_both(functools.partial(halo_copy, t))
    for copy in stores:
        copy.wait()

    lax.fori_loop(1, tiles, await_pick, 0)

    def gather(i, picked):
        return picked + recv_pick[i]

    picked = lax.fori_loop(1, tiles, gather, recv_pick[0])
    solved = jnp.sum(augmented[...] * picked, axis=0, keepdims=True)
    coef_ref[...] = solved[:, 0:nsrc]


def per_device(residual, kernel, dest_tile, cell_ids, wind_x, wind_y, mixing, sources, gram_matrix):
    tiles, groups = lax.axis_size("tile"), lax.axis_size("ens")
    members, levels, rows, columns = wind_x.shape
    blocks = cell_ids.shape[0]
    nsrc = gram_matrix.shape[0]
    strips = columns // LANES
    width = columns // groups
    flat = (members * levels * rows, columns)
    dims = (tiles, groups, members, levels, rows, columns, blocks)
    edge_rows = rows + 2 * (HALO - 1)
    state_rows = rows + 2 * HALO
    rounds = -(-STEPS // HALO)
    obs_rows = CAP * (levels + members + 2)
    span = min(GROUP, tiles) * CAP * LANES
    smem = pl.BlockSpec(memory_space=pltpu.SMEM)
    vmem = pl.BlockSpec(memory_space=pltpu.VMEM)
    anywhere = pl.BlockSpec(memory_space=pl.ANY)
    f32, bf16 = jnp.float32, jnp.bfloat16
    dma = pltpu.SemaphoreType.DMA
    gradient, coefficients, adjoint = pl.pallas_call(
        functools.partial(body, dims),
        out_shape=(
            jax.ShapeDtypeStruct((rows, width), f32),
            jax.ShapeDtypeStruct((1, nsrc), f32),
            jax.ShapeDtypeStruct(flat, f32),
        ),
        in_specs=[smem, smem] + [anywhere] * 7,
        out_specs=(vmem, vmem, anywhere),
        scratch_shapes=[
            pltpu.VMEM(residual.shape, f32),
            pltpu.VMEM(kernel.shape, f32),
            pltpu.VMEM(cell_ids.shape, jnp.int32),
            pltpu.VMEM(gram_matrix.shape, f32),
            pltpu.VMEM((3, strips, flat[0], LANES), f32),
            pltpu.VMEM((edge_rows, 4, members, levels, columns), f32),
            pltpu.VMEM((STEPS + 1, state_rows, members, levels, columns), f32),
            pltpu.VMEM((state_rows, levels, columns), f32),
            pltpu.VMEM((strips, flat[0], LANES), f32),
            pltpu.VMEM((tiles, obs_rows, LANES), f32),
            pltpu.VMEM((tiles, obs_rows, LANES), f32),
            pltpu.VMEM((rows * members * levels, span), bf16),
            pltpu.VMEM((rows * members * levels, span), bf16),
            pltpu.VMEM((columns, span), bf16),
            pltpu.VMEM((rows * members * levels, columns), f32),
            pltpu.VMEM((rows, columns), f32),
            pltpu.VMEM((nsrc, columns), f32),
            pltpu.VMEM((groups, rows + nsrc, width), f32),
            pltpu.VMEM((groups, rows + nsrc, width), f32),
            pltpu.VMEM((nsrc, width), f32),
            pltpu.VMEM((tiles, nsrc, width), f32),
            pltpu.VMEM((nsrc, LANES), f32),
            dma((4,)),
            dma((3, strips)),
            dma((tiles,)),
            dma((tiles,)),
            dma((2,)),
            dma((2,)),
            dma((2, rounds)),
            dma((2, rounds)),
            dma((groups,)),
            dma((groups,)),
            dma((tiles,)),
            dma((tiles,)),
            dma((strips,)),
        ],
        compiler_params=pltpu.CompilerParams(
            collective_id=0, has_side_effects=True, vmem_limit_bytes=63 * 1024 * 1024
        ),
        cost_estimate=pl.CostEstimate(
            flops=1_000_000_000, bytes_accessed=2_200_000, transcendentals=0
        ),
    )(
        dest_tile,
        sources,
        residual,
        kernel,
        cell_ids,
        gram_matrix,
        wind_x.reshape(flat),
        wind_y.reshape(flat),
        mixing.reshape(flat),
    )
    return gradient, coefficients.reshape(nsrc), adjoint.reshape(wind_x.shape)


def solution(mesh):
    in_specs = (
        P("ens", "tile", None),
        P("tile", None, None),
        P("tile", None),
        P("tile", None),
        P("ens", None, "tile", None),
        P("ens", None, "tile", None),
        P("ens", None, "tile", None),
        P(),
        P(),
    )
    out_specs = (P("tile", "ens"), P(), P("ens", None, "tile", None))
    return jax.shard_map(
        per_device, mesh=mesh, in_specs=in_specs, out_specs=out_specs, check_vma=False
    )
```

```python
import functools

import jax
import jax.numpy as jnp
from jax import lax
from jax.experimental import pallas as pl
from jax.experimental.pallas import tpu as pltpu
from jax.sharding import PartitionSpec as P

CAP = 2
STEPS = 6
HALO = 2
GROUP = 8
LANES = 128


def roll(array, shift, axis):
    return pltpu.roll(array, shift % array.shape[axis], axis=axis)


def body(
    dims,
    dest_ref,
    sources_ref,
    residual_hbm,
    kernel_hbm,
    cells_hbm,
    gram_hbm,
    wx_ref,
    wy_ref,
    mix_ref,
    grad_ref,
    coef_ref,
    adj_ref,
    residual_ref,
    kernel_ref,
    cells_ref,
    gram_ref,
    raw,
    coefs,
    states,
    total,
    outbuf,
    send_obs,
    recv_obs,
    left_hi,
    left_lo,
    right_hot,
    forcing,
    level0,
    picks,
    send_sum,
    recv_sum,
    send_pick,
    recv_pick,
    augmented,
    small_sem,
    local_sem,
    obs_send,
    obs_recv,
    edge_send,
    edge_recv,
    halo_send,
    halo_recv,
    sum_send,
    sum_recv,
    pick_send,
    pick_recv,
    out_sem,
):
    tiles, groups, members, levels, rows, columns, blocks = dims
    width = columns // groups
    strips = columns // LANES
    nsrc = gram_ref.shape[0]
    me = lax.axis_index("tile")
    mine = lax.axis_index("ens")
    depth = members * levels
    log_columns = columns.bit_length() - 1

    smalls = []
    pairs = (
        (residual_hbm, residual_ref),
        (kernel_hbm, kernel_ref),
        (cells_hbm, cells_ref),
        (gram_hbm, gram_ref),
    )
    for which, (source, target) in enumerate(pairs):
        copy = pltpu.make_async_copy(source, target, small_sem.at[which])
        copy.start()
        smalls.append(copy)

    loads = []
    for which, source in enumerate((wx_ref, wy_ref, mix_ref)):
        for j in range(strips):
            copy = pltpu.make_async_copy(
                source.at[:, pl.ds(j * LANES, LANES)],
                raw.at[which, j],
                local_sem.at[which, j],
            )
            copy.start()
            loads.append(copy)

    barrier = pltpu.get_barrier_semaphore()

    def greet_tile(d, carry):
        peer = lax.rem(me + d, tiles)
        pl.semaphore_signal(barrier, inc=1, device_id={"tile": peer})
        return carry

    def greet_ens(d, carry):
        peer = lax.rem(mine + d, groups)
        pl.semaphore_signal(barrier, inc=1, device_id={"ens": peer})
        return carry

    lax.fori_loop(1, tiles, greet_tile, 0)
    lax.fori_loop(1, groups, greet_ens, 0)

    for copy in smalls:
        copy.wait()

    def fill(tile, carry):
        def look(b, found):
            first, second = found
            here = dest_ref[b, 0] == tile
            second = jnp.where(here & (first >= 0) & (second < 0), b, second)
            first = jnp.where(here & (first < 0), b, first)
            return first, second

        none = jnp.int32(-1)
        found = lax.fori_loop(0, blocks, look, (none, none), unroll=min(blocks, 8))
        for c in range(CAP):
            block = jnp.maximum(found[c], 0)
            held = found[c] >= 0
            send_obs[tile, c * levels : (c + 1) * levels, :] = kernel_ref[block]
            base = CAP * levels + c * (members + 2)
            for m in range(members):
                part = residual_ref[m, pl.ds(block, 1), :]
                send_obs[tile, base + m : base + m + 1, :] = jnp.where(held, part, 0.0)
            ids = cells_ref[pl.ds(block, 1), :].astype(jnp.float32)
            send_obs[tile, base + members : base + members + 1, :] = ids
        return carry

    lax.fori_loop(0, tiles, fill, 0)

    pl.semaphore_wait(barrier, tiles + groups - 2)

    def obs_copy(d):
        peer = lax.rem(me + d, tiles)
        return pltpu.make_async_remote_copy(
            src_ref=send_obs.at[peer],
            dst_ref=recv_obs.at[me],
            send_sem=obs_send.at[d],
            recv_sem=obs_recv.at[d],
            device_id={"tile": peer},
        )

    def start_obs(d, carry):
        obs_copy(d).start()
        return carry

    lax.fori_loop(1, tiles, start_obs, 0)
    recv_obs[me] = send_obs[me]

    for t in range(0, STEPS + 1):

        @pl.when(me == 0)
        def _():
            states[t, 0:HALO] = jnp.zeros((HALO, members, levels, columns), jnp.float32)

        @pl.when(me == tiles - 1)
        def _():
            states[t, HALO + rows :] = jnp.zeros((HALO, members, levels, columns), jnp.float32)

    edge = HALO - 1
    if edge:

        @pl.when(me == 0)
        def _():
            coefs[0:edge] = jnp.zeros((edge,) + coefs.shape[1:], jnp.float32)

        @pl.when(me == tiles - 1)
        def _():
            coefs[edge + rows :] = jnp.zeros((edge,) + coefs.shape[1:], jnp.float32)

    for copy in loads:
        copy.wait()

    level_iota = lax.broadcasted_iota(jnp.int32, (levels, LANES), 0)
    lane_iota = lax.broadcasted_iota(jnp.int32, (levels, LANES), 1)

    def prepare(x, carry):
        made = []
        for m in range(members):
            at = pl.ds(m * levels * rows + x, levels, stride=rows)
            for j in range(strips):
                wx = raw[0, j, at, :]
                wy = raw[1, j, at, :]
                mixing = raw[2, j, at, :]
                center = 1.0 - jnp.abs(wx) - jnp.abs(wy)
                if j == 0:
                    wy = jnp.where((lane_iota == 0) & (wy < 0.0), 0.0, wy)
                if j == strips - 1:
                    wy = jnp.where((lane_iota == LANES - 1) & (wy > 0.0), 0.0, wy)
                mixing = jnp.where(level_iota == levels - 1, 0.0, mixing)
                made.append((m, j, (center, wx, wy, mixing)))
        for m, j, parts in made:
            for which, value in enumerate(parts):
                coefs[edge + x, which, m, :, j * LANES : (j + 1) * LANES] = value
        return carry

    lax.fori_loop(0, rows, prepare, 0)

    def edge_copy(upward):
        if upward:
            return pltpu.make_async_remote_copy(
                src_ref=coefs.at[pl.ds(rows, edge)],
                dst_ref=coefs.at[pl.ds(0, edge)],
                send_sem=edge_send.at[0],
                recv_sem=edge_recv.at[0],
                device_id={"tile": me + 1},
            )
        return pltpu.make_async_remote_copy(
            src_ref=coefs.at[pl.ds(edge, edge)],
            dst_ref=coefs.at[pl.ds(edge + rows, edge)],
            send_sem=edge_send.at[1],
            recv_sem=edge_recv.at[1],
            device_id={"tile": me - 1},
        )

    def halo_copy(t, upward):
        n = t // HALO
        if upward:
            return pltpu.make_async_remote_copy(
                src_ref=states.at[t, pl.ds(rows, HALO)],
                dst_ref=states.at[t, pl.ds(0, HALO)],
                send_sem=halo_send.at[0, n],
                recv_sem=halo_recv.at[0, n],
                device_id={"tile": me + 1},
            )
        return pltpu.make_async_remote_copy(
            src_ref=states.at[t, pl.ds(HALO, HALO)],
            dst_ref=states.at[t, pl.ds(HALO + rows, HALO)],
            send_sem=halo_send.at[1, n],
            recv_sem=halo_recv.at[1, n],
            device_id={"tile": me - 1},
        )

    def start_both(make):
        @pl.when(me < tiles - 1)
        def _():
            make(True).start()

        @pl.when(me > 0)
        def _():
            make(False).start()

    def await_both(make):
        @pl.when(me > 0)
        def _():
            make(True).wait_recv()

        @pl.when(me < tiles - 1)
        def _():
            make(False).wait_recv()

    def drain_both(make):
        @pl.when(me < tiles - 1)
        def _():
            make(True).wait_send()

        @pl.when(me > 0)
        def _():
            make(False).wait_send()

    if edge:
        start_both(edge_copy)

    row_iota = lax.broadcasted_iota(jnp.int32, (nsrc, LANES), 0)
    col_iota = lax.broadcasted_iota(jnp.int32, (nsrc, LANES), 1)
    augmented[...] = jnp.where(row_iota == col_iota, 1.0, 0.0)
    augmented[:, nsrc : 2 * nsrc] = gram_ref[...]

    def eliminate(first, stop):
        table = augmented[...]
        for i in range(first, stop):
            pivot = table[i : i + 1, :]
            scaled = pivot / table[i : i + 1, nsrc + i : nsrc + i + 1]
            column = table[:, nsrc + i : nsrc + i + 1]
            table = jnp.where(row_iota == i, scaled, table - column * scaled)
        augmented[...] = table

    def await_obs(d, carry):
        obs_copy(d).wait()
        return carry

    lax.fori_loop(1, tiles, await_obs, 0)

    group = min(GROUP, tiles)
    part_rows = LANES * CAP
    cell_rows = lax.broadcasted_iota(jnp.int32, (rows, depth, LANES), 0)
    cell_cols = lax.broadcasted_iota(jnp.int32, (columns, LANES), 0)

    def place(g, carry):
        for s in range(group):
            block = recv_obs[g * group + s]
            for c in range(CAP):
                at = s * part_rows + c * LANES
                base = CAP * levels + c * (members + 2)
                weights = block[c * levels : (c + 1) * levels]
                values = jnp.concatenate(
                    [weights * block[base + m : base + m + 1] for m in range(members)], axis=0
                )
                ids = block[base + members : base + members + 1].astype(jnp.int32)
                row = jnp.right_shift(ids, log_columns)
                col = jnp.bitwise_and(ids, columns - 1)
                high = values.astype(jnp.bfloat16).astype(jnp.float32)
                low = values - high
                inside = cell_rows == row[None]
                shape = (rows * depth, LANES)
                left_hi[:, at : at + LANES] = (
                    jnp.where(inside, high[None], 0.0).reshape(shape).astype(jnp.bfloat16)
                )
                left_lo[:, at : at + LANES] = (
                    jnp.where(inside, low[None], 0.0).reshape(shape).astype(jnp.bfloat16)
                )
                right_hot[:, at : at + LANES] = jnp.where(cell_cols == col, 1.0, 0.0).astype(
                    jnp.bfloat16
                )
        numbers = (((1,), (1,)), ((), ()))
        hot = right_hot[...]
        placed = lax.dot_general(left_hi[...], hot, numbers, preferred_element_type=jnp.float32)
        placed += lax.dot_general(left_lo[...], hot, numbers, preferred_element_type=jnp.float32)
        if group == tiles:
            forcing[...] = placed
        else:
            forcing[...] += placed
        return carry

    if group == tiles:
        place(0, 0)
    else:
        forcing[...] = jnp.zeros_like(forcing)
        lax.fori_loop(0, tiles // group, place, 0)
    states[0, HALO : HALO + rows] = forcing[...].reshape(rows, members, levels, columns)

    def advance_rows(t, chosen):
        last = t == STEPS - 1
        results = []
        for r in chosen:
            for m in range(members):
                here = states[t, r, m]
                above = states[t, r + 1, m]
                below = states[t, r - 1, m]
                center = coefs[r - 1, 0, m]
                wx = coefs[r - 1, 1, m]
                wy = coefs[r - 1, 2, m]
                mixing = coefs[r - 1, 3, m]
                right = roll(here, -1, 1)
                left = roll(here, 1, 1)
                flux = mixing * (roll(here, -1, 0) - here)
                new = center * here
                new += jnp.abs(wx) * jnp.where(wx > 0.0, above, below)
                new += jnp.abs(wy) * jnp.where(wy > 0.0, right, left)
                new += flux - roll(flux, 1, 0)
                results.append((r, m, new))
        sums = []
        for r in chosen:
            summed = sum(new for row, _, new in results if row is r)
            sums.append(summed + total[r] if t > 0 else summed)
        for r, summed in zip(chosen, sums):
            total[r] = summed
        for r, m, new in results:
            if last:
                at = pl.ds(m * levels * rows + r - HALO, levels, stride=rows)
                for j in range(strips):
                    outbuf[j, at, :] = new[:, j * LANES : (j + 1) * LANES]
            else:
                states[t + 1, r, m] = new

    def advance_span(t, first, stop):
        count = stop - first
        unroll = next(u for u in (4, 3, 2, 1) if count % u == 0)

        def one(i, carry):
            start = first + i * unroll
            advance_rows(t, [start + u for u in range(unroll)])
            return carry

        lax.fori_loop(0, count // unroll, one, 0)

    for t in range(STEPS):
        part = t % HALO
        reach = HALO - 1 - part
        if part == 0:
            start_both(functools.partial(halo_copy, t))
            advance_span(t, HALO + 1, HALO + rows - 1)
            if t == 0 and edge:
                await_both(edge_copy)
            await_both(functools.partial(halo_copy, t))
            advance_span(t, HALO - reach, HALO + 1)
            advance_span(t, HALO + rows - 1, HALO + rows + reach)
        else:
            advance_span(t, HALO - reach, HALO + rows + reach)

    stores = []
    for j in range(strips):
        copy = pltpu.make_async_copy(
            outbuf.at[j], adj_ref.at[:, pl.ds(j * LANES, LANES)], out_sem.at[j]
        )
        copy.start()
        stores.append(copy)

    for x in range(rows):
        level0[x : x + 1, :] = total[HALO + x, 0:1, :]
    for e in range(groups):
        send_sum[e, 0:rows, :] = level0[:, e * width : (e + 1) * width]
    wide_iota = lax.broadcasted_iota(jnp.int32, (1, columns), 1)
    for s in range(nsrc):
        place_of = sources_ref[s]
        row = jnp.right_shift(place_of, log_columns) - me * rows
        col = jnp.bitwise_and(place_of, columns - 1)
        inside = (row >= 0) & (row < rows)
        line = level0[pl.ds(jnp.clip(row, 0, rows - 1), 1), :]
        picks[s : s + 1, :] = jnp.where(wide_iota == jnp.where(inside, col, -1), line, 0.0)
    found = jnp.sum(picks[...], axis=1, keepdims=True)
    found = jnp.broadcast_to(found, (nsrc, width))
    for e in range(groups):
        send_sum[e, rows : rows + nsrc, :] = found

    def sum_copy(d):
        peer = lax.rem(mine + d, groups)
        return pltpu.make_async_remote_copy(
            src_ref=send_sum.at[peer],
            dst_ref=recv_sum.at[mine],
            send_sem=sum_send.at[d],
            recv_sem=sum_recv.at[d],
            device_id={"ens": peer},
        )

    for d in range(1, groups):
        sum_copy(d).start()
    recv_sum[mine] = send_sum[mine]
    eliminate(0, nsrc // 2)
    for d in range(1, groups):
        sum_copy(d).wait()
    summed = recv_sum[0]
    for e in range(1, groups):
        summed = summed + recv_sum[e]
    grad_ref[...] = summed[0:rows]
    send_pick[...] = summed[rows : rows + nsrc]

    def pick_copy(d):
        peer = lax.rem(me + d, tiles)
        return pltpu.make_async_remote_copy(
            src_ref=send_pick,
            dst_ref=recv_pick.at[me],
            send_sem=pick_send.at[d],
            recv_sem=pick_recv.at[d],
            device_id={"tile": peer},
        )

    def start_pick(d, carry):
        pick_copy(d).start()
        return carry

    def await_pick(d, carry):
        pick_copy(d).wait()
        return carry

    lax.fori_loop(1, tiles, start_pick, 0)
    recv_pick[me] = send_pick[...]
    eliminate(nsrc // 2, nsrc)

    if edge:
        drain_both(edge_copy)
    for t in range(0, STEPS, HALO):
        drain_both(functools.partial(halo_copy, t))
    for copy in stores:
        copy.wait()

    lax.fori_loop(1, tiles, await_pick, 0)

    def gather(i, picked):
        return picked + recv_pick[i]

    picked = lax.fori_loop(1, tiles, gather, recv_pick[0])
    solved = jnp.sum(augmented[...] * picked, axis=0, keepdims=True)
    coef_ref[...] = solved[:, 0:nsrc]


def per_device(residual, kernel, dest_tile, cell_ids, wind_x, wind_y, mixing, sources, gram_matrix):
    tiles, groups = lax.axis_size("tile"), lax.axis_size("ens")
    members, levels, rows, columns = wind_x.shape
    blocks = cell_ids.shape[0]
    nsrc = gram_matrix.shape[0]
    strips = columns // LANES
    width = columns // groups
    flat = (members * levels * rows, columns)
    dims = (tiles, groups, members, levels, rows, columns, blocks)
    edge_rows = rows + 2 * (HALO - 1)
    state_rows = rows + 2 * HALO
    rounds = -(-STEPS // HALO)
    obs_rows = CAP * (levels + members + 2)
    span = min(GROUP, tiles) * CAP * LANES
    smem = pl.BlockSpec(memory_space=pltpu.SMEM)
    vmem = pl.BlockSpec(memory_space=pltpu.VMEM)
    anywhere = pl.BlockSpec(memory_space=pl.ANY)
    f32, bf16 = jnp.float32, jnp.bfloat16
    dma = pltpu.SemaphoreType.DMA
    gradient, coefficients, adjoint = pl.pallas_call(
        functools.partial(body, dims),
        out_shape=(
            jax.ShapeDtypeStruct((rows, width), f32),
            jax.ShapeDtypeStruct((1, nsrc), f32),
            jax.ShapeDtypeStruct(flat, f32),
        ),
        in_specs=[smem, smem] + [anywhere] * 7,
        out_specs=(vmem, vmem, anywhere),
        scratch_shapes=[
            pltpu.VMEM(residual.shape, f32),
            pltpu.VMEM(kernel.shape, f32),
            pltpu.VMEM(cell_ids.shape, jnp.int32),
            pltpu.VMEM(gram_matrix.shape, f32),
            pltpu.VMEM((3, strips, flat[0], LANES), f32),
            pltpu.VMEM((edge_rows, 4, members, levels, columns), f32),
            pltpu.VMEM((STEPS + 1, state_rows, members, levels, columns), f32),
            pltpu.VMEM((state_rows, levels, columns), f32),
            pltpu.VMEM((strips, flat[0], LANES), f32),
            pltpu.VMEM((tiles, obs_rows, LANES), f32),
            pltpu.VMEM((tiles, obs_rows, LANES), f32),
            pltpu.VMEM((rows * members * levels, span), bf16),
            pltpu.VMEM((rows * members * levels, span), bf16),
            pltpu.VMEM((columns, span), bf16),
            pltpu.VMEM((rows * members * levels, columns), f32),
            pltpu.VMEM((rows, columns), f32),
            pltpu.VMEM((nsrc, columns), f32),
            pltpu.VMEM((groups, rows + nsrc, width), f32),
            pltpu.VMEM((groups, rows + nsrc, width), f32),
            pltpu.VMEM((nsrc, width), f32),
            pltpu.VMEM((tiles, nsrc, width), f32),
            pltpu.VMEM((nsrc, LANES), f32),
            dma((4,)),
            dma((3, strips)),
            dma((tiles,)),
            dma((tiles,)),
            dma((2,)),
            dma((2,)),
            dma((2, rounds)),
            dma((2, rounds)),
            dma((groups,)),
            dma((groups,)),
            dma((tiles,)),
            dma((tiles,)),
            dma((strips,)),
        ],
        compiler_params=pltpu.CompilerParams(
            collective_id=0, has_side_effects=True, vmem_limit_bytes=63 * 1024 * 1024
        ),
        cost_estimate=pl.CostEstimate(
            flops=1_000_000_000, bytes_accessed=2_200_000, transcendentals=0
        ),
    )(
        dest_tile,
        sources,
        residual,
        kernel,
        cell_ids,
        gram_matrix,
        wind_x.reshape(flat),
        wind_y.reshape(flat),
        mixing.reshape(flat),
    )
    return gradient, coefficients.reshape(nsrc), adjoint.reshape(wind_x.shape)


def solution(mesh):
    in_specs = (
        P("ens", "tile", None),
        P("tile", None, None),
        P("tile", None),
        P("tile", None),
        P("ens", None, "tile", None),
        P("ens", None, "tile", None),
        P("ens", None, "tile", None),
        P(),
        P(),
    )
    out_specs = (P("tile", "ens"), P(), P("ens", None, "tile", None))
    return jax.shard_map(
        per_device, mesh=mesh, in_specs=in_specs, out_specs=out_specs, check_vma=False
    )
```
